256 devices in a mesh: lev: 8 (over z), wave: 32 (over x, y, core).
Axes of the slice: x: 4, y: 4, z: 8, core: 2. Of those that a mesh axis runs over, the one named last changes fastest.
Arguments:
- grid: bfloat16 [512, 512, 1024], P(None, 'wave', 'lev'), may hold values from -6 to 6
- legendre: bfloat16 [512, 512, 512], P('wave'), may hold values from -0.25 to 0.25
- lengths: int32 [512], replicated, may hold values from 256 to 1024, as said below
- lat_order: int32 [512], replicated, may hold values from 0 to 511, each once
- wave_order: int32 [512], replicated, may hold values from 0 to 511, each once
Outputs:
- spectral: bfloat16 [512, 512, 2, 512], P('lev', 'wave')
The draws below stay inside these ranges and needn't reach their ends.
Inputs may be any that keep to these rules, and one draw needn't show every extreme that they name: `lengths`: at least 256, and 1024 on at least one latitude. `lat_order`: each latitude once. `wave_order`: each wavenumber once.
All inputs are finite; a program needn't handle non-finite values.
Results may differ from the reference program's by a relative error of at most 0.0058.
Values may be sent and summed in bfloat16 or wider, within the bound.
A program may use at most 128 MiB of HBM per device.

```python
import math
import jax
import jax.numpy as jnp
from jax import lax

NLAT = 512
NLON = 1024
TRUNC = 512
CHANNELS = 512


def draw_lengths(key, part):
    key = jax.random.fold_in(key, 7)
    first_key, second_key = jax.random.split(key)
    base = jax.random.randint(first_key, (NLAT,), NLON // 4, NLON + 1)
    widest = jax.random.randint(second_key, (), 0, NLAT)
    return jnp.where(jnp.arange(NLAT) == widest, NLON, base).astype(jnp.int32)


def levels(stream_key, extent, shards, least, high):
    def one(dim, parts):
        draws = jax.random.uniform(jax.random.fold_in(jax.random.fold_in(stream_key, 6), dim), (parts,), jnp.float32, least / len(shards), high / len(shards))
        return jnp.repeat(jnp.exp(draws), extent[dim] // parts).reshape((-1,) + (1,) * (len(extent) - dim - 1))

    factor_of = one(*shards[0])
    for cut in shards[1:]:
        factor_of = factor_of * one(*cut)
    return factor_of


def gaussian(own_key, shape, scale, reach, cuts=(), kind=jnp.bfloat16):
    result = scale * jax.random.normal(own_key, shape, jnp.float32)
    if cuts:
        result = result * levels(own_key, shape, cuts, -0.22, 0.18)
    return jnp.clip(result, -reach, reach).astype(kind)


def setup_inputs(seed: int = 0) -> dict:
    streams_of = jax.random.split(jax.random.key(seed), 6)
    return {
        "grid": gaussian(streams_of[0], (CHANNELS, NLAT, NLON), 1.0, 6.0, ((1, 32), (2, 8))),
        "legendre": gaussian(streams_of[1], (TRUNC, NLAT, TRUNC), NLAT ** -0.5, 0.25, ((0, 32),)),
        "lengths": draw_lengths(jax.random.fold_in(streams_of[5], 71), 0),
        "lat_order": jax.random.permutation(streams_of[3], NLAT).astype(jnp.int32),
        "wave_order": jax.random.permutation(streams_of[4], TRUNC).astype(jnp.int32),
    }


def trig_pair(phase, width):
    angle = 2.0 * math.pi * phase.astype(jnp.float32) / width
    return (jnp.cos(angle), jnp.sin(angle))

def row_table(length, wave_list, offset, count):
    width = length.astype(jnp.float32)
    factor = 1.0 / jnp.sqrt(width)
    waves = wave_list[None, :]
    columns = offset + jnp.arange(count, dtype=jnp.int32)
    if count % 32 == 0:
        highs = offset + 32 * jnp.arange(count // 32, dtype=jnp.int32)
        lows = jnp.arange(32, dtype=jnp.int32)
        high_cos, high_sin = trig_pair(highs[:, None] * waves % length, width)
        low_cos, low_sin = trig_pair(lows[:, None] * waves % length, width)
        real = high_cos[:, None, :] * low_cos[None, :, :] - high_sin[:, None, :] * low_sin[None, :, :]
        imag = high_sin[:, None, :] * low_cos[None, :, :] + high_cos[:, None, :] * low_sin[None, :, :]
        real = real.reshape(count, wave_list.shape[0])
        imag = imag.reshape(count, wave_list.shape[0])
    else:
        highs = columns // 32 * 32
        lows = columns % 32
        high_cos, high_sin = trig_pair(highs[:, None] * waves % length, width)
        low_cos, low_sin = trig_pair(lows[:, None] * waves % length, width)
        real = high_cos * low_cos - high_sin * low_sin
        imag = high_sin * low_cos + high_cos * low_sin
    inside = columns[:, None] < length
    cosines = jnp.where(inside, real * factor, 0.0)
    sines = jnp.where(inside, -imag * factor, 0.0)
    return jnp.concatenate([cosines, sines], axis=1).astype(jnp.bfloat16)

def reference(grid, legendre, lengths, lat_order, wave_order):
    row_lengths = lengths[lat_order]

    def one_row(position):
        block = lax.dynamic_index_in_dim(grid, position, 1, keepdims=False)
        length = lax.dynamic_index_in_dim(row_lengths, position, 0, keepdims=False)
        table = row_table(length, wave_order, 0, NLON)
        return jnp.dot(block, table, preferred_element_type=jnp.float32).astype(jnp.bfloat16)
    fourier = lax.map(one_row, jnp.arange(NLAT, dtype=jnp.int32))
    fourier = fourier.reshape(NLAT, CHANNELS, 2, TRUNC)
    inverse = jnp.zeros((NLAT,), jnp.int32).at[lat_order].set(jnp.arange(NLAT, dtype=jnp.int32))
    by_latitude = jnp.take(fourier, inverse, axis=0)
    degrees = jnp.arange(TRUNC, dtype=jnp.int32)

    def one_slot(slot):
        weights = lax.dynamic_index_in_dim(legendre, slot, 0, keepdims=False).astype(jnp.float32)
        column = lax.dynamic_index_in_dim(by_latitude, slot, 3, keepdims=False).astype(jnp.float32)
        total = jnp.einsum('lkc,ln->kcn', column, weights)
        order = lax.dynamic_index_in_dim(wave_order, slot, 0, keepdims=False)
        return jnp.where(degrees[None, None, :] >= order, total, 0.0).astype(jnp.bfloat16)
    spectral = lax.map(one_slot, jnp.arange(TRUNC, dtype=jnp.int32))
    return jnp.transpose(spectral, (1, 0, 2, 3))
```

```python
import functools
import math

import jax
import jax.numpy as jnp
from jax import lax
from jax.experimental import pallas as pl
from jax.experimental.pallas import tpu as pltpu
from jax.sharding import PartitionSpec as P

MESH = pl.DeviceIdType.MESH
BF16 = jnp.bfloat16
F32 = jnp.float32

LEVS = 8
WAVES = 32
ROWS = 16
SLOTS = 16
KEEP = 64
NLAT = 512
DEG = 512
NWAVE = 512
LANES = 128

CHUNKS = (4, 4, 4, 2, 2)
STARTS = tuple(sum(CHUNKS[:i]) for i in range(len(CHUNKS)))
LAST = len(CHUNKS) - 1
ZORDER = (4, 3, 5, 2, 6, 1, 7)

SIN_C = tuple((-1) ** i * math.pi ** (2 * i + 1) / math.factorial(2 * i + 1) for i in range(7))
COS_C = tuple((-1) ** i * math.pi ** (2 * i) / math.factorial(2 * i) for i in range(8))


def iota(shape, dim):
    return lax.broadcasted_iota(jnp.int32, shape, dim)


def horner(coefs, u):
    acc = jnp.full_like(u, coefs[-1])
    for c in coefs[-2::-1]:
        acc = acc * u + c
    return acc


def turn(count, width, inverse):
    whole = jnp.floor(count * inverse + 0.5)
    t = (count - whole * width) * inverse
    u = t * t
    s = t * horner(SIN_C, u)
    c = horner(COS_C, u)
    return 1.0 - 2.0 * s * s, 2.0 * s * c


def nt_dot(a, b):
    return lax.dot_general(a, b, (((1,), (1,)), ((), ())), preferred_element_type=F32)


def dot(a, b):
    return jnp.dot(a, b, preferred_element_type=F32)


def kernel(grid_hbm, leg_hbm, len_s, lat_s, wave_s, lat_v, wave_v, out_ref,
           gin, g, x, table, fs, fr, a, lraw, lp, acc, onehot, swap, mcol,
           gin_sem, leg_sem, zs, zr, ws, wr):
    z = lax.axis_index("lev")
    w = lax.axis_index("wave")
    bar = pltpu.get_barrier_semaphore()

    def signal_z(i, carry):
        pl.semaphore_signal(bar, inc=1, device_id=(lax.rem(z + i, LEVS), w), device_id_type=MESH)
        return carry

    def signal_w(i, carry):
        pl.semaphore_signal(bar, inc=1, device_id=(z, lax.rem(w + i, WAVES)), device_id_type=MESH)
        return carry

    lax.fori_loop(1, LEVS, signal_z, 0)
    lax.fori_loop(1, WAVES, signal_w, 0)
    grid_copy = pltpu.make_async_copy(grid_hbm, gin, gin_sem)
    grid_copy.start()
    leg_copy = pltpu.make_async_copy(leg_hbm, lraw, leg_sem)
    leg_copy.start()

    i = iota((256, 256), 0)
    j = iota((256, 256), 1)
    swap[...] = jnp.where(j == (i % 16) * 16 + i // 16, 1.0, 0.0).astype(BF16)

    grid_copy.wait()

    def to_rows(blk, carry):
        k0 = pl.multiple_of(blk * 16, 16)
        v = gin[pl.ds(k0, 16)].reshape(256, LANES)
        v = dot(swap[...], v).astype(BF16).reshape(16, 16, LANES)
        d = blk // 4
        kk = pl.multiple_of(lax.rem(blk, 4) * 16, 16)
        for c, rows in enumerate(CHUNKS):
            r0 = STARTS[c]
            g[pl.ds(LEVS * r0 + d * rows, rows), pl.ds(kk, 16), :] = v[r0 : r0 + rows]
        return carry

    lax.fori_loop(0, 32, to_rows, 0)
    pl.semaphore_wait(bar, LEVS - 1 + WAVES - 1)

    for c, rows in enumerate(CHUNKS):
        base = LEVS * STARTS[c]
        for o in ZORDER:
            p = lax.rem(z + o, LEVS)
            pltpu.make_async_remote_copy(
                src_ref=g.at[pl.ds(base + p * rows, rows)],
                dst_ref=x.at[pl.ds(base + z * rows, rows)],
                send_sem=zs.at[c], recv_sem=zr.at[c],
                device_id=(p, w), device_id_type=MESH,
            ).start()
    for c, rows in enumerate(CHUNKS):
        own = pl.ds(LEVS * STARTS[c] + z * rows, rows)
        x[own] = g[own]

    col = jnp.zeros((NWAVE, LANES), F32)
    for t in range(4):
        hit = iota((NWAVE, LANES), 1) + LANES * t == iota((NWAVE, LANES), 0)
        col = col + jnp.where(hit, wave_v[t : t + 1, :].astype(F32), 0.0)
    mcol[...] = jnp.broadcast_to(jnp.sum(col, axis=1, keepdims=True), (NWAVE, LANES))
    for c, rows in enumerate(CHUNKS):
        n = WAVES * rows
        q = iota((n, LANES), 0)
        row = (q // rows) * ROWS + STARTS[c] + q % rows
        col = jnp.zeros((n, LANES), F32)
        for t in range(4):
            hit = iota((n, LANES), 1) + LANES * t == row
            col = col + jnp.where(hit, lat_v[t : t + 1, :].astype(F32), 0.0)
        lat = jnp.sum(col, axis=1, keepdims=True)
        onehot[WAVES * STARTS[c] : WAVES * STARTS[c] + n, :] = jnp.where(
            iota((n, NLAT), 1).astype(F32) == lat, 1.0, 0.0
        ).astype(BF16)

    def make_table(r0, rows):
        def one(rr, carry):
            length = len_s[lat_s[w * ROWS + r0 + rr]]
            width = jnp.full((1, LANES), length, jnp.int32).astype(F32)
            inverse = 1.0 / width
            factor = 1.0 / jnp.sqrt(width)

            def block(b, carry2):
                s0 = pl.multiple_of(b * 64, 64)
                m = mcol[pl.ds(s0, 64), :]
                low = iota((64, LANES), 1).astype(F32)
                c0, s0_ = turn(m * low, width, inverse)
                dc, ds = turn(m * float(LANES), width, inverse)
                c0 = c0 * factor
                s0_ = s0_ * (-factor)
                c1 = c0 * dc + s0_ * ds
                s1 = s0_ * dc - c0 * ds
                two = 2.0 * dc
                for d in range(LEVS):
                    table[rr, pl.ds(s0, 64), d * LANES : (d + 1) * LANES] = c0.astype(BF16)
                    table[rr, pl.ds(s0, 64), (LEVS + d) * LANES : (LEVS + d + 1) * LANES] = s0_.astype(BF16)
                    if d < LEVS - 1:
                        c0, c1 = c1, two * c1 - c0
                        s0_, s1 = s1, two * s1 - s0_
                return carry2

            lax.fori_loop(0, NWAVE // 64, block, 0)
            return carry

        lax.fori_loop(0, rows, one, 0)

    def transform(r0, rows):
        def one(rr, carry):
            length = len_s[lat_s[w * ROWS + r0 + rr]]
            parts = []
            for d in range(LEVS):
                inside = iota((KEEP, LANES), 1) + d * LANES < length
                keep = jnp.where(inside, 1.0, 0.0).astype(BF16)
                parts.append(x[LEVS * r0 + d * rows + rr] * keep)
            line = jnp.concatenate(parts, axis=1)
            zero = jnp.zeros_like(line)
            real = jnp.concatenate([line, zero], axis=0)
            imag = jnp.concatenate([zero, line], axis=0)
            f = nt_dot(table[rr, :, : LEVS * LANES], real)
            f = f + nt_dot(table[rr, :, LEVS * LANES :], imag)
            f = f.astype(BF16)
            for p in range(WAVES):
                fs[WAVES * r0 + p * rows + rr] = f[SLOTS * p : SLOTS * (p + 1)]
            return carry

        lax.fori_loop(0, rows, one, 0)

    def send_wave(c):
        rows = CHUNKS[c]
        base = WAVES * STARTS[c]

        def one(o, carry):
            px = lax.rem(w // 8 + o // 8, 4)
            py = lax.rem(lax.rem(w // 2, 4) + lax.rem(o // 2, 4), 4)
            pc = lax.rem(lax.rem(w, 2) + lax.rem(o, 2), 2)
            p = px * 8 + py * 2 + pc
            pltpu.make_async_remote_copy(
                src_ref=fs.at[pl.ds(base + p * rows, rows)],
                dst_ref=fr.at[pl.ds(base + w * rows, rows)],
                send_sem=ws.at[c], recv_sem=wr.at[c],
                device_id=(z, p), device_id_type=MESH,
            ).start()
            return carry

        lax.fori_loop(1, WAVES, one, 0)
        own = pl.ds(base + w * rows, rows)
        fr[own] = fs[own]

    def z_all(c):
        region = pl.ds(LEVS * STARTS[c], (LEVS - 1) * CHUNKS[c])
        return pltpu.make_async_remote_copy(
            src_ref=g.at[region], dst_ref=x.at[region], send_sem=zs.at[c], recv_sem=zr.at[c],
            device_id=(lax.rem(z + 1, LEVS), w), device_id_type=MESH)

    def wave_all(c):
        region = pl.ds(WAVES * STARTS[c], (WAVES - 1) * CHUNKS[c])
        return pltpu.make_async_remote_copy(
            src_ref=fs.at[region], dst_ref=fr.at[region], send_sem=ws.at[c], recv_sem=wr.at[c],
            device_id=(z, lax.rem(w + 1, WAVES)), device_id_type=MESH)

    def to_slots(c):
        first = WAVES * STARTS[c] // 16

        def one(b, carry):
            q = pl.multiple_of(b * 16, 16)
            v = fr[pl.ds(q, 16)].reshape(256, LANES)
            a[:, pl.ds(q, 16), :] = dot(swap[...], v).astype(BF16).reshape(16, 16, LANES)
            return carry

        lax.fori_loop(first, first + 2 * CHUNKS[c], one, 0)

    make_table(0, CHUNKS[0])

    leg_copy.wait()

    def order_legendre(s, carry):
        m = wave_s[w * SLOTS + s]
        for h in range(2):
            cols = slice(256 * h, 256 * (h + 1))
            keep = iota((256, 256), 1) + 256 * h >= m
            for q in range(2):
                rows = slice(256 * q, 256 * (q + 1))
                v = dot(onehot[rows, :], lraw[s, :, cols])
                lp[s, rows, cols] = jnp.where(keep, v, 0.0).astype(BF16)
        return carry

    lax.fori_loop(0, SLOTS, order_legendre, 0)

    for c in range(len(CHUNKS)):
        z_all(c).wait_recv()
        transform(STARTS[c], CHUNKS[c])
        send_wave(c)
        if c < LAST:
            make_table(STARTS[c + 1], CHUNKS[c + 1])
        if c > 0:
            wave_all(c - 1).wait_recv()
            to_slots(c - 1)

    i = iota((LANES, LANES), 0)
    j = iota((LANES, LANES), 1)
    order = jnp.where(j == (i % 2) * KEEP + i // 2, 1.0, 0.0).astype(BF16)
    cut = WAVES * STARTS[LAST]

    def sum_first(s, carry):
        at = nt_dot(order, a[s, :cut, :]).astype(BF16)
        acc[s] = dot(at, lp[s, :cut, :])
        return carry

    lax.fori_loop(0, SLOTS, sum_first, 0)

    wave_all(LAST).wait_recv()
    to_slots(LAST)

    def sum_last(s, carry):
        at = nt_dot(order, a[s, cut:, :]).astype(BF16)
        total = acc[s] + dot(at, lp[s, cut:, :])
        out_ref[:, s] = total.astype(BF16).reshape(KEEP, 2, DEG)
        return carry

    lax.fori_loop(0, SLOTS, sum_last, 0)

    for c in range(len(CHUNKS)):
        z_all(c).wait_send()
        wave_all(c).wait_send()


def on_device(grid, legendre, lengths, lat_order, wave_order):
    any_spec = pl.BlockSpec(memory_space=pl.ANY)
    smem = pl.BlockSpec(memory_space=pltpu.SMEM)
    vmem = pl.BlockSpec(memory_space=pltpu.VMEM)
    n = len(CHUNKS)
    dma = pltpu.SemaphoreType.DMA
    return pl.pallas_call(
        kernel,
        out_shape=jax.ShapeDtypeStruct((KEEP, SLOTS, 2, DEG), BF16),
        in_specs=[any_spec, any_spec, smem, smem, smem, vmem, vmem],
        out_specs=vmem,
        scratch_shapes=[
            pltpu.VMEM((512, ROWS, LANES), BF16),
            pltpu.VMEM((LEVS * ROWS, KEEP, LANES), BF16),
            pltpu.VMEM((LEVS * ROWS, KEEP, LANES), BF16),
            pltpu.VMEM((max(CHUNKS), NWAVE, 2 * LEVS * LANES), BF16),
            pltpu.VMEM((WAVES * ROWS, SLOTS, LANES), BF16),
            pltpu.VMEM((WAVES * ROWS, SLOTS, LANES), BF16),
            pltpu.VMEM((SLOTS, NLAT, LANES), BF16),
            pltpu.VMEM((SLOTS, NLAT, DEG), BF16),
            pltpu.VMEM((SLOTS, NLAT, DEG), BF16),
            pltpu.VMEM((SLOTS, LANES, DEG), F32),
            pltpu.VMEM((NLAT, NLAT), BF16),
            pltpu.VMEM((256, 256), BF16),
            pltpu.VMEM((NWAVE, LANES), F32),
            dma, dma, dma((n,)), dma((n,)), dma((n,)), dma((n,)),
        ],
        compiler_params=pltpu.CompilerParams(
            collective_id=0, has_side_effects=True, vmem_limit_bytes=58 << 20
        ),
        cost_estimate=pl.CostEstimate(flops=14 * 10**9, bytes_accessed=14 << 20, transcendentals=0),
    )(grid, legendre, lengths, lat_order, wave_order, lat_order.reshape(4, 128), wave_order.reshape(4, 128))


def solution(mesh):
    return jax.shard_map(
        on_device,
        mesh=mesh,
        in_specs=(P(None, "wave", "lev"), P("wave", None, None), P(), P(), P()),
        out_specs=P("lev", "wave", None, None),
        check_vma=False,
    )
```

```python
import jax
import jax.numpy as jnp
from jax import lax
from jax.experimental import pallas as pl
from jax.experimental.pallas import tpu as pltpu
from jax.sharding import PartitionSpec as P

MESH = pl.DeviceIdType.MESH
BF16 = jnp.bfloat16
F32 = jnp.float32

LEVS = 8
WAVES = 32
ROWS = 16
SLOTS = 16
KEEP = 64
NLAT = 512
DEG = 512
NWAVE = 512
LANES = 128

CHUNKS = (4, 4, 4, 2, 1, 1)
STARTS = tuple(sum(CHUNKS[:i]) for i in range(len(CHUNKS)))
LAST = len(CHUNKS) - 1
CUT = WAVES * STARTS[LAST]
ZORDER = (4, 3, 5, 2, 6, 1, 7)

SIN_C = (3.14159264, -5.16771008, 2.55007752, -0.59829129, 0.07765766)
COS_C = (0.99999995, -4.93479283, 4.05841135, -1.33187657, 0.21968961)


def iota(shape, dim):
    return lax.broadcasted_iota(jnp.int32, shape, dim)


def horner(coefs, u):
    acc = u * coefs[-1] + coefs[-2]
    for c in coefs[-3::-1]:
        acc = acc * u + c
    return acc


def turn(count, width, inverse):
    whole = jnp.floor(count * inverse + 0.5)
    t = (count - whole * width) * inverse
    u = t * t
    s = t * horner(SIN_C, u)
    c = horner(COS_C, u)
    s2 = s + s
    return 1.0 - s2 * s, s2 * c


def nt_dot(a, b):
    return lax.dot_general(a, b, (((1,), (1,)), ((), ())), preferred_element_type=F32)


def dot(a, b):
    return jnp.dot(a, b, preferred_element_type=F32)


def set_swap(swap):
    i = iota((256, 256), 0)
    j = iota((256, 256), 1)
    swap[...] = jnp.where(j == (i % 16) * 16 + i // 16, 1.0, 0.0).astype(BF16)


def part_last():
    i = iota((LANES, LANES), 0)
    j = iota((LANES, LANES), 1)
    return jnp.where(j == (i % 2) * KEEP + i // 2, 1.0, 0.0).astype(BF16)


def kernel(grid_hbm, leg_hbm, len_s, lat_s, wave_s, lat_v, wave_v, acc, lp_last, fr_last,
           gin, g, x, table, turns, both, fs, fr, a, lraw, lp, onehot, swap, mcol,
           gin_sem, leg_sem, zs, zr, ws, wr):
    z = lax.axis_index("lev")
    w = lax.axis_index("wave")
    bar = pltpu.get_barrier_semaphore()

    def signal_z(i, carry):
        pl.semaphore_signal(bar, inc=1, device_id=(lax.rem(z + i, LEVS), w), device_id_type=MESH)
        return carry

    def signal_w(i, carry):
        pl.semaphore_signal(bar, inc=1, device_id=(z, lax.rem(w + i, WAVES)), device_id_type=MESH)
        return carry

    lax.fori_loop(1, LEVS, signal_z, 0)
    lax.fori_loop(1, WAVES, signal_w, 0)
    visit = ZORDER + (0,)

    def grid_copy(i):
        part = pl.ds(lax.rem(z + visit[i], LEVS) * KEEP, KEEP)
        return pltpu.make_async_copy(grid_hbm.at[part], gin.at[part], gin_sem.at[i])

    for i in range(LEVS):
        grid_copy(i).start()
    leg_copy = pltpu.make_async_copy(leg_hbm, lraw, leg_sem)
    leg_copy.start()

    set_swap(swap)

    def send_z(c, p):
        rows = CHUNKS[c]
        base = LEVS * STARTS[c]
        pltpu.make_async_remote_copy(
            src_ref=g.at[pl.ds(base + p * rows, rows)],
            dst_ref=x.at[pl.ds(base + z * rows, rows)],
            send_sem=zs.at[c], recv_sem=zr.at[c],
            device_id=(p, w), device_id_type=MESH,
        ).start()

    for i in range(LEVS):
        grid_copy(i).wait()
        p = lax.rem(z + visit[i], LEVS)
        for pair in range(2):
            k0 = pl.multiple_of(p * KEEP + pair * 32, 32)
            v = jnp.concatenate([gin[pl.ds(k0 + 16 * h, 16)].reshape(256, LANES) for h in range(2)], axis=1)
            v = dot(swap[...], v).astype(BF16)
            for h in range(2):
                kk = pair * 32 + 16 * h
                part = v[:, LANES * h : LANES * (h + 1)].reshape(16, 16, LANES)
                for c, rows in enumerate(CHUNKS):
                    r0 = STARTS[c]
                    dest = g if i < LEVS - 1 else x
                    dest[pl.ds(LEVS * r0 + p * rows, rows), kk : kk + 16, :] = part[r0 : r0 + rows]
        if i == 0:
            pl.semaphore_wait(bar, LEVS - 1 + WAVES - 1)
        if i < LEVS - 1:
            send_z(0, p)
    for c in range(1, len(CHUNKS)):
        for o in ZORDER:
            send_z(c, lax.rem(z + o, LEVS))

    col = jnp.zeros((NWAVE, LANES), F32)
    for t in range(4):
        hit = iota((NWAVE, LANES), 1) + LANES * t == iota((NWAVE, LANES), 0)
        col = col + jnp.where(hit, wave_v[t : t + 1, :].astype(F32), 0.0)
    mcol[...] = jnp.broadcast_to(jnp.sum(col, axis=1, keepdims=True), (NWAVE, LANES))
    for c, rows in enumerate(CHUNKS):
        n = WAVES * rows
        q = iota((n, LANES), 0)
        row = (q // rows) * ROWS + STARTS[c] + q % rows
        col = jnp.zeros((n, LANES), F32)
        for t in range(4):
            hit = iota((n, LANES), 1) + LANES * t == row
            col = col + jnp.where(hit, lat_v[t : t + 1, :].astype(F32), 0.0)
        lat = jnp.sum(col, axis=1, keepdims=True)
        onehot[WAVES * STARTS[c] : WAVES * STARTS[c] + n, :] = jnp.where(
            iota((n, NLAT), 1).astype(F32) == lat, 1.0, 0.0
        ).astype(BF16)

    def make_table(r0, rows):
        def one(rr, carry):
            length = len_s[lat_s[w * ROWS + r0 + rr]]
            width = jnp.full((1, LANES), length, jnp.int32).astype(F32)
            inverse = 1.0 / width
            factor = 1.0 / jnp.sqrt(width)
            lane = iota((32, LANES), 1)
            left = lane < KEEP
            low = lane.astype(F32)

            def block(b, carry2):
                s0 = pl.multiple_of(b * 32, 32)
                rows_c = pl.ds(s0, 32)
                rows_s = pl.ds(NWAVE + s0, 32)
                m = mcol[rows_c, :]
                cl, sl = turn(m * low, width, inverse)
                table[rr, rows_c, :LANES] = cl.astype(BF16)
                table[rr, rows_s, :LANES] = sl.astype(BF16)
                c1, s1 = turn(m * float(LANES), width, inverse)
                table[rr, rows_c, LANES:] = (cl * c1 - sl * s1).astype(BF16)
                table[rr, rows_s, LANES:] = (sl * c1 + cl * s1).astype(BF16)
                t = s1 + s1
                c2, s2 = 1.0 - t * s1, t * c1
                t = s2 + s2
                c4, s4 = factor - t * (s2 * factor), t * (c2 * factor)
                turns[rr, rows_c, :LANES] = jnp.where(left, 1.0, c2) * factor
                turns[rr, rows_s, :LANES] = jnp.where(left, 0.0, s2) * factor
                turns[rr, rows_c, LANES:] = jnp.where(left, c4, c4 * c2 - s4 * s2)
                turns[rr, rows_s, LANES:] = jnp.where(left, s4, s4 * c2 + c4 * s2)
                return carry2

            lax.fori_loop(0, NWAVE // 32, block, 0, unroll=2)
            return carry

        lax.fori_loop(0, rows, one, 0)

    def transform(r0, rows):
        left = iota((32, LANES), 1) < KEEP

        def one(rr, carry):
            length = len_s[lat_s[w * ROWS + r0 + rr]]
            parts = []
            for d in range(LEVS):
                inside = iota((KEEP, LANES), 1) + d * LANES < length
                keep = jnp.where(inside, 1.0, 0.0).astype(BF16)
                parts.append(x[LEVS * r0 + d * rows + rr] * keep)
            lines = jnp.concatenate(
                [jnp.concatenate(parts[2 * d : 2 * d + 2], axis=1) for d in range(4)], axis=0
            )
            both[...] = nt_dot(table[rr], lines)
            for b in range(NWAVE // 32):
                rows_c = slice(32 * b, 32 * (b + 1))
                rows_s = slice(NWAVE + 32 * b, NWAVE + 32 * (b + 1))
                real, imag = 0.0, 0.0
                for t in range(2):
                    cols = slice(LANES * t, LANES * (t + 1))
                    u, v = both[rows_c, cols], both[rows_s, cols]
                    c, q = turns[rr, rows_c, cols], turns[rr, rows_s, cols]
                    real = real + (c * u - q * v)
                    imag = imag - (q * u + c * v)
                f = jnp.where(left, real, pltpu.roll(imag, KEEP, axis=1))
                f = f + jnp.where(left, pltpu.roll(real, KEEP, axis=1), imag)
                f = f.astype(BF16)
                for i in range(2):
                    fs[WAVES * r0 + (2 * b + i) * rows + rr] = f[SLOTS * i : SLOTS * (i + 1)]
            return carry

        lax.fori_loop(0, rows, one, 0)

    def landing(c, first, count):
        if c == LAST:
            return fr_last.at[pl.ds(first, count)]
        return fr.at[pl.ds(WAVES * STARTS[c] + first, count)]

    def send_wave(c):
        rows = CHUNKS[c]
        base = WAVES * STARTS[c]

        def one(o, carry):
            px = lax.rem(w // 8 + o // 8, 4)
            py = lax.rem(lax.rem(w // 2, 4) + lax.rem(o // 2, 4), 4)
            pc = lax.rem(lax.rem(w, 2) + lax.rem(o, 2), 2)
            p = px * 8 + py * 2 + pc
            pltpu.make_async_remote_copy(
                src_ref=fs.at[pl.ds(base + p * rows, rows)],
                dst_ref=landing(c, w * rows, rows),
                send_sem=ws.at[c], recv_sem=wr.at[c],
                device_id=(z, p), device_id_type=MESH,
            ).start()
            return carry

        lax.fori_loop(1, WAVES, one, 0)
        own = pl.ds(base + w * rows, rows)
        if c == LAST:
            fr_last[pl.ds(w * rows, rows)] = fs[own]
        else:
            fr[own] = fs[own]

    def z_all(c):
        region = pl.ds(LEVS * STARTS[c], (LEVS - 1) * CHUNKS[c])
        return pltpu.make_async_remote_copy(
            src_ref=g.at[region], dst_ref=x.at[region], send_sem=zs.at[c], recv_sem=zr.at[c],
            device_id=(lax.rem(z + 1, LEVS), w), device_id_type=MESH)

    def wave_all(c):
        region = pl.ds(WAVES * STARTS[c], (WAVES - 1) * CHUNKS[c])
        return pltpu.make_async_remote_copy(
            src_ref=fs.at[region], dst_ref=landing(c, 0, (WAVES - 1) * CHUNKS[c]),
            send_sem=ws.at[c], recv_sem=wr.at[c],
            device_id=(z, lax.rem(w + 1, WAVES)), device_id_type=MESH)

    def to_slots(c):
        first = WAVES * STARTS[c] // 32

        def one(b, carry):
            q = pl.multiple_of(b * 32, 32)
            v = jnp.concatenate([fr[pl.ds(q + 16 * h, 16)].reshape(256, LANES) for h in range(2)], axis=1)
            v = dot(swap[...], v).astype(BF16)
            for h in range(2):
                a[:, pl.ds(q + 16 * h, 16), :] = v[:, LANES * h : LANES * (h + 1)].reshape(16, 16, LANES)
            return carry

        lax.fori_loop(first, first + CHUNKS[c], one, 0, unroll=2)

    make_table(0, CHUNKS[0])

    leg_copy.wait()

    def order_legendre(s, carry):
        m = wave_s[w * SLOTS + s]
        for h in range(2):
            cols = slice(256 * h, 256 * (h + 1))
            keep = iota((256, 256), 1) + 256 * h >= m
            for q in range(2):
                rows = slice(256 * q, 256 * (q + 1))
                v = dot(onehot[rows, :], lraw[s, :, cols])
                lp[s, rows, cols] = jnp.where(keep, v, 0.0).astype(BF16)
        return carry

    lax.fori_loop(0, SLOTS, order_legendre, 0)

    lp_last[...] = lp[:, CUT:, :]

    for c in range(len(CHUNKS)):
        z_all(c).wait_recv()
        transform(STARTS[c], CHUNKS[c])
        send_wave(c)
        if c < LAST:
            make_table(STARTS[c + 1], CHUNKS[c + 1])
        if c > 0:
            wave_all(c - 1).wait_recv()
            to_slots(c - 1)

    order = part_last()

    def sum_first(s, carry):
        at = nt_dot(order, a[s, :, :]).astype(BF16)
        acc[s] = dot(at, lp[s, :CUT, :])
        return carry

    lax.fori_loop(0, SLOTS, sum_first, 0, unroll=4)

    wave_all(LAST).wait_recv()

    for c in range(len(CHUNKS)):
        z_all(c).wait_send()
        wave_all(c).wait_send()


def finish(acc, lp, fr, out_ref, a, swap):
    tail = NLAT - CUT
    group = out_ref.shape[1]

    @pl.when(pl.program_id(0) == 0)
    def _():
        set_swap(swap)
        for b in range(tail // 32):
            v = jnp.concatenate([fr[32 * b + 16 * h : 32 * b + 16 * h + 16].reshape(256, LANES) for h in range(2)], axis=1)
            v = dot(swap[...], v).astype(BF16)
            for h in range(2):
                q = 32 * b + 16 * h
                a[:, q : q + 16, :] = v[:, LANES * h : LANES * (h + 1)].reshape(16, 16, LANES)

    first = pl.multiple_of(pl.program_id(0) * group, group)
    slots = pl.ds(first, group)
    at = nt_dot(part_last(), a[slots].reshape(group * tail, LANES)).astype(BF16)
    weights = lp[slots].reshape(group * tail, DEG)
    slot = iota((LANES, group * tail), 1) // tail
    for s in range(group):
        own = jnp.where(slot == s, 1.0, 0.0).astype(BF16)
        total = acc[first + s] + dot(at * own, weights)
        out_ref[:, s] = total.astype(BF16).reshape(KEEP, 2, DEG)


def on_device(grid, legendre, lengths, lat_order, wave_order):
    any_spec = pl.BlockSpec(memory_space=pl.ANY)
    smem = pl.BlockSpec(memory_space=pltpu.SMEM)
    vmem = pl.BlockSpec(memory_space=pltpu.VMEM)
    n = len(CHUNKS)
    dma = pltpu.SemaphoreType.DMA
    tail = NLAT - CUT
    group = 4
    acc, lp, fr = pl.pallas_call(
        kernel,
        out_shape=[
            pltpu.VMEM((SLOTS, 2 * KEEP, DEG), F32),
            pltpu.VMEM((SLOTS, tail, DEG), BF16),
            pltpu.VMEM((tail, SLOTS, LANES), BF16),
        ],
        in_specs=[any_spec, any_spec, smem, smem, smem, vmem, vmem],
        out_specs=[vmem] * 3,
        scratch_shapes=[
            pltpu.VMEM((512, ROWS, LANES), BF16),
            pltpu.VMEM((LEVS * ROWS, KEEP, LANES), BF16),
            pltpu.VMEM((LEVS * ROWS, KEEP, LANES), BF16),
            pltpu.VMEM((max(CHUNKS), 2 * NWAVE, 2 * LANES), BF16),
            pltpu.VMEM((max(CHUNKS), 2 * NWAVE, 2 * LANES), F32),
            pltpu.VMEM((2 * NWAVE, 2 * LANES), F32),
            pltpu.VMEM((WAVES * ROWS, SLOTS, LANES), BF16),
            pltpu.VMEM((CUT, SLOTS, LANES), BF16),
            pltpu.VMEM((SLOTS, CUT, LANES), BF16),
            pltpu.VMEM((SLOTS, NLAT, DEG), BF16),
            pltpu.VMEM((SLOTS, NLAT, DEG), BF16),
            pltpu.VMEM((NLAT, NLAT), BF16),
            pltpu.VMEM((256, 256), BF16),
            pltpu.VMEM((NWAVE, LANES), F32),
            dma((LEVS,)), dma, dma((n,)), dma((n,)), dma((n,)), dma((n,)),
        ],
        compiler_params=pltpu.CompilerParams(
            collective_id=0, has_side_effects=True, vmem_limit_bytes=55 << 20
        ),
        cost_estimate=pl.CostEstimate(flops=14 * 10**9, bytes_accessed=14 << 20, transcendentals=0),
    )(grid, legendre, lengths, lat_order, wave_order, lat_order.reshape(4, 128), wave_order.reshape(4, 128))
    return pl.pallas_call(
        finish,
        grid=(SLOTS // group,),
        out_shape=jax.ShapeDtypeStruct((KEEP, SLOTS, 2, DEG), BF16),
        in_specs=[vmem] * 3,
        out_specs=pl.BlockSpec((KEEP, group, 2, DEG), lambda i: (0, i, 0, 0)),
        scratch_shapes=[pltpu.VMEM((SLOTS, tail, LANES), BF16), pltpu.VMEM((256, 256), BF16)],
        compiler_params=pltpu.CompilerParams(vmem_limit_bytes=32 << 20),
    )(acc, lp, fr)


def solution(mesh):
    return jax.shard_map(
        on_device,
        mesh=mesh,
        in_specs=(P(None, "wave", "lev"), P("wave", None, None), P(), P(), P()),
        out_specs=P("lev", "wave", None, None),
        check_vma=False,
    )
```

```python
import jax
import jax.numpy as jnp
from jax import lax
from jax.experimental import pallas as pl
from jax.experimental.pallas import tpu as pltpu
from jax.sharding import PartitionSpec as P

MESH = pl.DeviceIdType.MESH
BF16 = jnp.bfloat16
F32 = jnp.float32

LEVS = 8
WAVES = 32
ROWS = 16
SLOTS = 16
KEEP = 64
NLAT = 512
DEG = 512
NWAVE = 512
LANES = 128

CHUNKS = (4, 4, 4, 2, 1, 1)
STARTS = tuple(sum(CHUNKS[:i]) for i in range(len(CHUNKS)))
LAST = len(CHUNKS) - 1
CUT = WAVES * STARTS[LAST]
HEAD = 256
TABLES = 8
ZORDER = (4, 3, 5, 2, 6, 1, 7)

SIN_C = (3.14159264, -5.16771008, 2.55007752, -0.59829129, 0.07765766)
COS_C = (0.99999995, -4.93479283, 4.05841135, -1.33187657, 0.21968961)


def iota(shape, dim):
    return lax.broadcasted_iota(jnp.int32, shape, dim)


def horner(coefs, u):
    acc = u * coefs[-1] + coefs[-2]
    for c in coefs[-3::-1]:
        acc = acc * u + c
    return acc


def turn(count, width, inverse):
    whole = jnp.floor(count * inverse + 0.5)
    t = (count - whole * width) * inverse
    u = t * t
    s = t * horner(SIN_C, u)
    c = horner(COS_C, u)
    s2 = s + s
    return 1.0 - s2 * s, s2 * c


def nt_dot(a, b):
    return lax.dot_general(a, b, (((1,), (1,)), ((), ())), preferred_element_type=F32)


def dot(a, b):
    return jnp.dot(a, b, preferred_element_type=F32)


def set_swap(swap):
    i = iota((256, 256), 0)
    j = iota((256, 256), 1)
    swap[...] = jnp.where(j == (i % 16) * 16 + i // 16, 1.0, 0.0).astype(BF16)


def part_last():
    i = iota((LANES, LANES), 0)
    j = iota((LANES, LANES), 1)
    return jnp.where(j == (i % 2) * KEEP + i // 2, 1.0, 0.0).astype(BF16)


def kernel(grid_hbm, leg_hbm, len_s, lat_s, wave_s, lat_v, wave_v, acc, lp_tail, a_tail, fr_last,
           gin, g, x, table, turns, both, fs, fr, a_head, lraw, lp_head, onehot, swap, mcol,
           gin_sem, leg_sem, zs, zr, ws, wr):
    z = lax.axis_index("lev")
    w = lax.axis_index("wave")
    bar = pltpu.get_barrier_semaphore()

    def signal_z(i, carry):
        pl.semaphore_signal(bar, inc=1, device_id=(lax.rem(z + i, LEVS), w), device_id_type=MESH)
        return carry

    def signal_w(i, carry):
        pl.semaphore_signal(bar, inc=1, device_id=(z, lax.rem(w + i, WAVES)), device_id_type=MESH)
        return carry

    lax.fori_loop(1, LEVS, signal_z, 0)
    lax.fori_loop(1, WAVES, signal_w, 0)
    visit = ZORDER + (0,)

    def grid_copy(i):
        part = pl.ds(lax.rem(z + visit[i], LEVS) * KEEP, KEEP)
        return pltpu.make_async_copy(grid_hbm.at[part], gin.at[part], gin_sem.at[i])

    for i in range(LEVS):
        grid_copy(i).start()
    leg_copy = pltpu.make_async_copy(leg_hbm, lraw, leg_sem)
    leg_copy.start()

    set_swap(swap)

    def send_z(c, p):
        rows = CHUNKS[c]
        base = LEVS * STARTS[c]
        pltpu.make_async_remote_copy(
            src_ref=g.at[pl.ds(base + p * rows, rows)],
            dst_ref=x.at[pl.ds(base + z * rows, rows)],
            send_sem=zs.at[c], recv_sem=zr.at[c],
            device_id=(p, w), device_id_type=MESH,
        ).start()

    for i in range(LEVS):
        grid_copy(i).wait()
        p = lax.rem(z + visit[i], LEVS)
        for pair in range(2):
            k0 = pl.multiple_of(p * KEEP + pair * 32, 32)
            v = jnp.concatenate([gin[pl.ds(k0 + 16 * h, 16)].reshape(256, LANES) for h in range(2)], axis=1)
            v = dot(swap[...], v).astype(BF16)
            for h in range(2):
                kk = pair * 32 + 16 * h
                part = v[:, LANES * h : LANES * (h + 1)].reshape(16, 16, LANES)
                for c, rows in enumerate(CHUNKS):
                    r0 = STARTS[c]
                    dest = g if i < LEVS - 1 else x
                    dest[pl.ds(LEVS * r0 + p * rows, rows), kk : kk + 16, :] = part[r0 : r0 + rows]
        if i == 0:
            pl.semaphore_wait(bar, LEVS - 1 + WAVES - 1)
        if i < LEVS - 1:
            send_z(0, p)
    for c in range(1, len(CHUNKS)):
        for o in ZORDER:
            send_z(c, lax.rem(z + o, LEVS))

    col = jnp.zeros((NWAVE, LANES), F32)
    for t in range(4):
        hit = iota((NWAVE, LANES), 1) + LANES * t == iota((NWAVE, LANES), 0)
        col = col + jnp.where(hit, wave_v[t : t + 1, :].astype(F32), 0.0)
    mcol[...] = jnp.broadcast_to(jnp.sum(col, axis=1, keepdims=True), (NWAVE, LANES))
    for c, rows in enumerate(CHUNKS):
        n = WAVES * rows
        q = iota((n, LANES), 0)
        row = (q // rows) * ROWS + STARTS[c] + q % rows
        col = jnp.zeros((n, LANES), F32)
        for t in range(4):
            hit = iota((n, LANES), 1) + LANES * t == row
            col = col + jnp.where(hit, lat_v[t : t + 1, :].astype(F32), 0.0)
        lat = jnp.sum(col, axis=1, keepdims=True)
        onehot[WAVES * STARTS[c] : WAVES * STARTS[c] + n, :] = jnp.where(
            iota((n, NLAT), 1).astype(F32) == lat, 1.0, 0.0
        ).astype(BF16)

    def make_table(r0, rows):
        def one(rr, carry):
            held = r0 % TABLES + rr
            length = len_s[lat_s[w * ROWS + r0 + rr]]
            width = jnp.full((1, LANES), length, jnp.int32).astype(F32)
            inverse = 1.0 / width
            factor = 1.0 / jnp.sqrt(width)
            lane = iota((32, LANES), 1)
            left = lane < KEEP
            low = lane.astype(F32)

            def block(b, carry2):
                s0 = pl.multiple_of(b * 32, 32)
                rows_c = pl.ds(s0, 32)
                rows_s = pl.ds(NWAVE + s0, 32)
                m = mcol[rows_c, :]
                cl, sl = turn(m * low, width, inverse)
                table[held, rows_c, :LANES] = cl.astype(BF16)
                table[held, rows_s, :LANES] = sl.astype(BF16)
                c1, s1 = turn(m * float(LANES), width, inverse)
                table[held, rows_c, LANES:] = (cl * c1 - sl * s1).astype(BF16)
                table[held, rows_s, LANES:] = (sl * c1 + cl * s1).astype(BF16)
                t = s1 + s1
                c2, s2 = 1.0 - t * s1, t * c1
                t = s2 + s2
                c4, s4 = factor - t * (s2 * factor), t * (c2 * factor)
                turns[held, rows_c, :LANES] = jnp.where(left, 1.0, c2) * factor
                turns[held, rows_s, :LANES] = jnp.where(left, 0.0, s2) * factor
                turns[held, rows_c, LANES:] = jnp.where(left, c4, c4 * c2 - s4 * s2)
                turns[held, rows_s, LANES:] = jnp.where(left, s4, s4 * c2 + c4 * s2)
                return carry2

            lax.fori_loop(0, NWAVE // 32, block, 0, unroll=2)
            return carry

        lax.fori_loop(0, rows, one, 0)

    def transform(r0, rows):
        left = iota((32, LANES), 1) < KEEP

        def one(rr, carry):
            length = len_s[lat_s[w * ROWS + r0 + rr]]
            held = r0 % TABLES + rr
            parts = []
            for d in range(LEVS):
                inside = iota((KEEP, LANES), 1) + d * LANES < length
                keep = jnp.where(inside, 1.0, 0.0).astype(BF16)
                parts.append(x[LEVS * r0 + d * rows + rr] * keep)
            lines = jnp.concatenate(
                [jnp.concatenate(parts[2 * d : 2 * d + 2], axis=1) for d in range(4)], axis=0
            )
            both[...] = nt_dot(table[held], lines)
            for b in range(NWAVE // 32):
                rows_c = slice(32 * b, 32 * (b + 1))
                rows_s = slice(NWAVE + 32 * b, NWAVE + 32 * (b + 1))
                real, imag = 0.0, 0.0
                for t in range(2):
                    cols = slice(LANES * t, LANES * (t + 1))
                    u, v = both[rows_c, cols], both[rows_s, cols]
                    c, q = turns[held, rows_c, cols], turns[held, rows_s, cols]
                    real = real + (c * u - q * v)
                    imag = imag - (q * u + c * v)
                f = jnp.where(left, real, pltpu.roll(imag, KEEP, axis=1))
                f = f + jnp.where(left, pltpu.roll(real, KEEP, axis=1), imag)
                f = f.astype(BF16)
                for i in range(2):
                    fs[WAVES * r0 + (2 * b + i) * rows + rr] = f[SLOTS * i : SLOTS * (i + 1)]
            return carry

        lax.fori_loop(0, rows, one, 0)

    def landing(c, first, count):
        if c == LAST:
            return fr_last.at[pl.ds(first, count)]
        return fr.at[pl.ds(WAVES * STARTS[c] + first, count)]

    def send_wave(c):
        rows = CHUNKS[c]
        base = WAVES * STARTS[c]

        def one(o, carry):
            px = lax.rem(w // 8 + o // 8, 4)
            py = lax.rem(lax.rem(w // 2, 4) + lax.rem(o // 2, 4), 4)
            pc = lax.rem(lax.rem(w, 2) + lax.rem(o, 2), 2)
            p = px * 8 + py * 2 + pc
            pltpu.make_async_remote_copy(
                src_ref=fs.at[pl.ds(base + p * rows, rows)],
                dst_ref=landing(c, w * rows, rows),
                send_sem=ws.at[c], recv_sem=wr.at[c],
                device_id=(z, p), device_id_type=MESH,
            ).start()
            return carry

        lax.fori_loop(1, WAVES, one, 0)
        own = pl.ds(base + w * rows, rows)
        if c == LAST:
            fr_last[pl.ds(w * rows, rows)] = fs[own]
        else:
            fr[own] = fs[own]

    def z_all(c):
        region = pl.ds(LEVS * STARTS[c], (LEVS - 1) * CHUNKS[c])
        return pltpu.make_async_remote_copy(
            src_ref=g.at[region], dst_ref=x.at[region], send_sem=zs.at[c], recv_sem=zr.at[c],
            device_id=(lax.rem(z + 1, LEVS), w), device_id_type=MESH)

    def wave_all(c):
        region = pl.ds(WAVES * STARTS[c], (WAVES - 1) * CHUNKS[c])
        return pltpu.make_async_remote_copy(
            src_ref=fs.at[region], dst_ref=landing(c, 0, (WAVES - 1) * CHUNKS[c]),
            send_sem=ws.at[c], recv_sem=wr.at[c],
            device_id=(z, lax.rem(w + 1, WAVES)), device_id_type=MESH)

    def to_slots(c):
        begin = WAVES * STARTS[c]
        dest, skip = (a_head, 0) if begin < HEAD else (a_tail, HEAD)

        def one(b, carry):
            q = pl.multiple_of(b * 32, 32)
            v = jnp.concatenate([fr[pl.ds(q + 16 * h, 16)].reshape(256, LANES) for h in range(2)], axis=1)
            v = dot(swap[...], v).astype(BF16)
            for h in range(2):
                to = pl.ds(q - skip + 16 * h, 16)
                dest[:, to, :] = v[:, LANES * h : LANES * (h + 1)].reshape(16, 16, LANES)
            return carry

        lax.fori_loop(begin // 32, begin // 32 + CHUNKS[c], one, 0, unroll=min(2, CHUNKS[c]))

    make_table(0, CHUNKS[0])

    leg_copy.wait()

    def order_legendre(s, carry):
        m = wave_s[w * SLOTS + s]
        for h in range(2):
            cols = slice(256 * h, 256 * (h + 1))
            keep = iota((256, 256), 1) + 256 * h >= m
            for q in range(2):
                rows = slice(256 * q, 256 * (q + 1))
                v = dot(onehot[rows, :], lraw[s, :, cols])
                part = lp_head if q == 0 else lp_tail
                part[s, :, cols] = jnp.where(keep, v, 0.0).astype(BF16)
        return carry

    lax.fori_loop(0, SLOTS, order_legendre, 0)

    def arrive(c):
        z_all(c).wait_recv()
        transform(STARTS[c], CHUNKS[c])
        send_wave(c)

    def collect(c):
        wave_all(c).wait_recv()
        to_slots(c)

    make_table(STARTS[1], CHUNKS[1])
    arrive(0)
    make_table(STARTS[2], CHUNKS[2])
    arrive(1)
    make_table(STARTS[3], ROWS - STARTS[3])
    collect(0)
    arrive(2)
    collect(1)

    order = part_last()

    def sum_first(s, carry):
        at = nt_dot(order, a_head[s]).astype(BF16)
        acc[s] = dot(at, lp_head[s])
        return carry

    lax.fori_loop(0, SLOTS, sum_first, 0, unroll=4)

    for c in range(3, LAST + 1):
        arrive(c)
    for c in range(2, LAST):
        collect(c)
    wave_all(LAST).wait_recv()

    for c in range(len(CHUNKS)):
        z_all(c).wait_send()
        wave_all(c).wait_send()


def finish(acc, lp_tail, a_tail, fr, out_ref, a, swap):
    group = out_ref.shape[1]
    tail = NLAT - HEAD
    ready = CUT - HEAD

    @pl.when(pl.program_id(0) == 0)
    def _():
        set_swap(swap)
        v = jnp.concatenate([fr[16 * h : 16 * h + 16].reshape(256, LANES) for h in range(2)], axis=1)
        v = dot(swap[...], v).astype(BF16)
        for h in range(2):
            a[:, ready + 16 * h : ready + 16 * h + 16, :] = v[:, LANES * h : LANES * (h + 1)].reshape(16, 16, LANES)
        a[:, :ready, :] = a_tail[...]

    first = pl.multiple_of(pl.program_id(0) * group, group)
    at = nt_dot(part_last(), a[pl.ds(first, group)].reshape(group * tail, LANES)).astype(BF16)
    for s in range(group):
        total = acc[first + s] + dot(at[:, tail * s : tail * (s + 1)], lp_tail[first + s])
        out_ref[:, s] = total.astype(BF16).reshape(KEEP, 2, DEG)


def on_device(grid, legendre, lengths, lat_order, wave_order):
    any_spec = pl.BlockSpec(memory_space=pl.ANY)
    smem = pl.BlockSpec(memory_space=pltpu.SMEM)
    vmem = pl.BlockSpec(memory_space=pltpu.VMEM)
    n = len(CHUNKS)
    dma = pltpu.SemaphoreType.DMA
    group = 4
    parts = pl.pallas_call(
        kernel,
        out_shape=[
            pltpu.VMEM((SLOTS, 2 * KEEP, DEG), F32),
            pltpu.VMEM((SLOTS, NLAT - HEAD, DEG), BF16),
            pltpu.VMEM((SLOTS, CUT - HEAD, LANES), BF16),
            pltpu.VMEM((NLAT - CUT, SLOTS, LANES), BF16),
        ],
        in_specs=[any_spec, any_spec, smem, smem, smem, vmem, vmem],
        out_specs=[vmem] * 4,
        scratch_shapes=[
            pltpu.VMEM((512, ROWS, LANES), BF16),
            pltpu.VMEM((LEVS * ROWS, KEEP, LANES), BF16),
            pltpu.VMEM((LEVS * ROWS, KEEP, LANES), BF16),
            pltpu.VMEM((TABLES, 2 * NWAVE, 2 * LANES), BF16),
            pltpu.VMEM((TABLES, 2 * NWAVE, 2 * LANES), F32),
            pltpu.VMEM((2 * NWAVE, 2 * LANES), F32),
            pltpu.VMEM((WAVES * ROWS, SLOTS, LANES), BF16),
            pltpu.VMEM((CUT, SLOTS, LANES), BF16),
            pltpu.VMEM((SLOTS, HEAD, LANES), BF16),
            pltpu.VMEM((SLOTS, NLAT, DEG), BF16),
            pltpu.VMEM((SLOTS, HEAD, DEG), BF16),
            pltpu.VMEM((NLAT, NLAT), BF16),
            pltpu.VMEM((256, 256), BF16),
            pltpu.VMEM((NWAVE, LANES), F32),
            dma((LEVS,)), dma, dma((n,)), dma((n,)), dma((n,)), dma((n,)),
        ],
        compiler_params=pltpu.CompilerParams(
            collective_id=0, has_side_effects=True, vmem_limit_bytes=51 << 20
        ),
        cost_estimate=pl.CostEstimate(flops=14 * 10**9, bytes_accessed=14 << 20, transcendentals=0),
    )(grid, legendre, lengths, lat_order, wave_order, lat_order.reshape(4, 128), wave_order.reshape(4, 128))
    return pl.pallas_call(
        finish,
        grid=(SLOTS // group,),
        out_shape=jax.ShapeDtypeStruct((KEEP, SLOTS, 2, DEG), BF16),
        in_specs=[vmem] * 4,
        out_specs=pl.BlockSpec((KEEP, group, 2, DEG), lambda i: (0, i, 0, 0)),
        scratch_shapes=[pltpu.VMEM((SLOTS, NLAT - HEAD, LANES), BF16), pltpu.VMEM((256, 256), BF16)],
        compiler_params=pltpu.CompilerParams(vmem_limit_bytes=32 << 20),
    )(*parts)


def solution(mesh):
    return jax.shard_map(
        on_device,
        mesh=mesh,
        in_specs=(P(None, "wave", "lev"), P("wave", None, None), P(), P(), P()),
        out_specs=P("lev", "wave", None, None),
        check_vma=False,
    )
```

```python
import jax
import jax.numpy as jnp
from jax import lax
from jax.experimental import pallas as pl
from jax.experimental.pallas import tpu as pltpu
from jax.sharding import PartitionSpec as P

MESH = pl.DeviceIdType.MESH
BF16 = jnp.bfloat16
F32 = jnp.float32

LEVS = 8
WAVES = 32
ROWS = 16
SLOTS = 16
KEEP = 64
NLAT = 512
DEG = 512
NWAVE = 512
LANES = 128

CHUNKS = (4, 4, 4, 2, 1, 1)
STARTS = tuple(sum(CHUNKS[:i]) for i in range(len(CHUNKS)))
LAST = len(CHUNKS) - 1
CUT = WAVES * STARTS[LAST]
HEAD = 256
TABLES = 8
ZORDER = (4, 3, 5, 2, 6, 1, 7)

SIN_C = (3.14159264, -5.16771008, 2.55007752, -0.59829129, 0.07765766)
COS_C = (0.99999995, -4.93479283, 4.05841135, -1.33187657, 0.21968961)


def iota(shape, dim):
    return lax.broadcasted_iota(jnp.int32, shape, dim)


def horner(coefs, u):
    acc = u * coefs[-1] + coefs[-2]
    for c in coefs[-3::-1]:
        acc = acc * u + c
    return acc


def turn(count, width, inverse):
    whole = jnp.floor(count * inverse + 0.5)
    t = (count - whole * width) * inverse
    u = t * t
    s = t * horner(SIN_C, u)
    c = horner(COS_C, u)
    s2 = s + s
    return 1.0 - s2 * s, s2 * c


def nt_dot(a, b):
    return lax.dot_general(a, b, (((1,), (1,)), ((), ())), preferred_element_type=F32)


def dot(a, b):
    return jnp.dot(a, b, preferred_element_type=F32)


def set_swap(swap):
    i = iota((256, 256), 0)
    j = iota((256, 256), 1)
    swap[...] = jnp.where(j == (i & 15) * 16 + (i >> 4), 1.0, 0.0).astype(BF16)


def part_last():
    i = iota((LANES, LANES), 0)
    j = iota((LANES, LANES), 1)
    return jnp.where(j == (i & 1) * KEEP + (i >> 1), 1.0, 0.0).astype(BF16)


def kernel(grid_hbm, leg_hbm, len_hbm, lat_hbm, wave_hbm, lat4_hbm, wave4_hbm, acc, lp_tail, a_tail, fr_last,
           gin, g, x, table, turns, both, fs, fr, a_head, lraw, lp_head, onehot, swap, mcol,
           len_s, lat_s, wave_s, lat_v, wave_v, gin_sem, leg_sem, small_sem, zs, zr, ws, wr):
    z = lax.axis_index("lev")
    w = lax.axis_index("wave")
    bar = pltpu.get_barrier_semaphore()

    def signal_z(i, carry):
        pl.semaphore_signal(bar, inc=1, device_id=(lax.rem(z + i, LEVS), w), device_id_type=MESH)
        return carry

    def signal_w(i, carry):
        pl.semaphore_signal(bar, inc=1, device_id=(z, lax.rem(w + i, WAVES)), device_id_type=MESH)
        return carry

    visit = ZORDER + (0,)

    def grid_copy(i):
        part = pl.ds(lax.rem(z + visit[i], LEVS) * KEEP, KEEP)
        return pltpu.make_async_copy(grid_hbm.at[part], gin.at[part], gin_sem.at[i])

    for i in range(LEVS):
        grid_copy(i).start()
    lax.fori_loop(1, LEVS, signal_z, 0)
    lax.fori_loop(1, WAVES, signal_w, 0)
    small = [
        pltpu.make_async_copy(src, dst, small_sem.at[i])
        for i, (src, dst) in enumerate(
            [(len_hbm, len_s), (lat_hbm, lat_s), (wave_hbm, wave_s), (lat4_hbm, lat_v), (wave4_hbm, wave_v)]
        )
    ]
    for copy in small:
        copy.start()
    leg_copy = pltpu.make_async_copy(leg_hbm, lraw, leg_sem)
    leg_copy.start()

    set_swap(swap)

    def send_z(c, p):
        rows = CHUNKS[c]
        base = LEVS * STARTS[c]
        pltpu.make_async_remote_copy(
            src_ref=g.at[pl.ds(base + p * rows, rows)],
            dst_ref=x.at[pl.ds(base + z * rows, rows)],
            send_sem=zs.at[c], recv_sem=zr.at[c],
            device_id=(p, w), device_id_type=MESH,
        ).start()

    for i in range(LEVS):
        grid_copy(i).wait()
        p = lax.rem(z + visit[i], LEVS)
        for pair in range(2):
            k0 = pl.multiple_of(p * KEEP + pair * 32, 32)
            v = jnp.concatenate([gin[pl.ds(k0 + 16 * h, 16)].reshape(256, LANES) for h in range(2)], axis=1)
            v = dot(swap[...], v).astype(BF16)
            for h in range(2):
                kk = pair * 32 + 16 * h
                part = v[:, LANES * h : LANES * (h + 1)].reshape(16, 16, LANES)
                for c, rows in enumerate(CHUNKS):
                    r0 = STARTS[c]
                    dest = g if i < LEVS - 1 else x
                    dest[pl.ds(LEVS * r0 + p * rows, rows), kk : kk + 16, :] = part[r0 : r0 + rows]
        if i == 0:
            pl.semaphore_wait(bar, LEVS - 1 + WAVES - 1)
        if i < LEVS - 1:
            send_z(0, p)
    for c in range(1, len(CHUNKS)):
        for o in ZORDER:
            send_z(c, lax.rem(z + o, LEVS))

    for copy in small:
        copy.wait()
    col = jnp.zeros((NWAVE, LANES), F32)
    for t in range(4):
        hit = iota((NWAVE, LANES), 1) + LANES * t == iota((NWAVE, LANES), 0)
        col = col + jnp.where(hit, wave_v[t : t + 1, :].astype(F32), 0.0)
    mcol[...] = jnp.broadcast_to(jnp.sum(col, axis=1, keepdims=True), (NWAVE, LANES))
    for c, rows in enumerate(CHUNKS):
        n = WAVES * rows
        q = iota((n, LANES), 0)
        row = (q // rows) * ROWS + STARTS[c] + q % rows
        col = jnp.zeros((n, LANES), F32)
        for t in range(4):
            hit = iota((n, LANES), 1) + LANES * t == row
            col = col + jnp.where(hit, lat_v[t : t + 1, :].astype(F32), 0.0)
        lat = jnp.sum(col, axis=1, keepdims=True)
        onehot[WAVES * STARTS[c] : WAVES * STARTS[c] + n, :] = jnp.where(
            iota((n, NLAT), 1).astype(F32) == lat, 1.0, 0.0
        ).astype(BF16)

    def make_table(r0, rows):
        def one(rr, carry):
            held = r0 % TABLES + rr
            length = len_s[lat_s[w * ROWS + r0 + rr]]
            width = jnp.full((1, LANES), length, jnp.int32).astype(F32)
            inverse = 1.0 / width
            factor = 1.0 / jnp.sqrt(width)
            lane = iota((32, LANES), 1)
            left = lane < KEEP
            low = lane.astype(F32)

            def block(b, carry2):
                s0 = pl.multiple_of(b * 32, 32)
                rows_c = pl.ds(s0, 32)
                rows_s = pl.ds(NWAVE + s0, 32)
                m = mcol[rows_c, :]
                cl, sl = turn(m * low, width, inverse)
                table[held, rows_c, :LANES] = cl.astype(BF16)
                table[held, rows_s, :LANES] = sl.astype(BF16)
                c1, s1 = turn(m * float(LANES), width, inverse)
                table[held, rows_c, LANES:] = (cl * c1 - sl * s1).astype(BF16)
                table[held, rows_s, LANES:] = (sl * c1 + cl * s1).astype(BF16)
                t = s1 + s1
                c2, s2 = 1.0 - t * s1, t * c1
                t = s2 + s2
                c4, s4 = factor - t * (s2 * factor), t * (c2 * factor)
                turns[held, rows_c, :LANES] = jnp.where(left, 1.0, c2) * factor
                turns[held, rows_s, :LANES] = jnp.where(left, 0.0, s2) * factor
                turns[held, rows_c, LANES:] = jnp.where(left, c4, c4 * c2 - s4 * s2)
                turns[held, rows_s, LANES:] = jnp.where(left, s4, s4 * c2 + c4 * s2)
                return carry2

            lax.fori_loop(0, NWAVE // 32, block, 0, unroll=2)
            return carry

        lax.fori_loop(0, rows, one, 0)

    def transform(r0, rows):
        left = iota((32, LANES), 1) < KEEP

        def one(rr, carry):
            length = len_s[lat_s[w * ROWS + r0 + rr]]
            held = r0 % TABLES + rr
            parts = []
            for d in range(LEVS):
                inside = iota((KEEP, LANES), 1) + d * LANES < length
                keep = jnp.where(inside, 1.0, 0.0).astype(BF16)
                parts.append(x[LEVS * r0 + d * rows + rr] * keep)
            lines = jnp.concatenate(
                [jnp.concatenate(parts[2 * d : 2 * d + 2], axis=1) for d in range(4)], axis=0
            )
            both[...] = nt_dot(table[held], lines)
            for b in range(NWAVE // 32):
                rows_c = slice(32 * b, 32 * (b + 1))
                rows_s = slice(NWAVE + 32 * b, NWAVE + 32 * (b + 1))
                real, imag = 0.0, 0.0
                for t in range(2):
                    cols = slice(LANES * t, LANES * (t + 1))
                    u, v = both[rows_c, cols], both[rows_s, cols]
                    c, q = turns[held, rows_c, cols], turns[held, rows_s, cols]
                    real = real + (c * u - q * v)
                    imag = imag - (q * u + c * v)
                f = jnp.where(left, real, pltpu.roll(imag, KEEP, axis=1))
                f = f + jnp.where(left, pltpu.roll(real, KEEP, axis=1), imag)
                f = f.astype(BF16)
                for i in range(2):
                    fs[WAVES * r0 + (2 * b + i) * rows + rr] = f[SLOTS * i : SLOTS * (i + 1)]
            return carry

        lax.fori_loop(0, rows, one, 0)

    def landing(c, first, count):
        if c == LAST:
            return fr_last.at[pl.ds(first, count)]
        return fr.at[pl.ds(WAVES * STARTS[c] + first, count)]

    def send_wave(c):
        rows = CHUNKS[c]
        base = WAVES * STARTS[c]

        def one(o, carry):
            px = lax.rem(w // 8 + o // 8, 4)
            py = lax.rem(lax.rem(w // 2, 4) + lax.rem(o // 2, 4), 4)
            pc = lax.rem(lax.rem(w, 2) + lax.rem(o, 2), 2)
            p = px * 8 + py * 2 + pc
            pltpu.make_async_remote_copy(
                src_ref=fs.at[pl.ds(base + p * rows, rows)],
                dst_ref=landing(c, w * rows, rows),
                send_sem=ws.at[c], recv_sem=wr.at[c],
                device_id=(z, p), device_id_type=MESH,
            ).start()
            return carry

        lax.fori_loop(1, WAVES, one, 0, unroll=c == LAST)
        own = pl.ds(base + w * rows, rows)
        if c == LAST:
            fr_last[pl.ds(w * rows, rows)] = fs[own]
        else:
            fr[own] = fs[own]

    def z_all(c):
        region = pl.ds(LEVS * STARTS[c], (LEVS - 1) * CHUNKS[c])
        return pltpu.make_async_remote_copy(
            src_ref=g.at[region], dst_ref=x.at[region], send_sem=zs.at[c], recv_sem=zr.at[c],
            device_id=(lax.rem(z + 1, LEVS), w), device_id_type=MESH)

    def wave_all(c):
        region = pl.ds(WAVES * STARTS[c], (WAVES - 1) * CHUNKS[c])
        return pltpu.make_async_remote_copy(
            src_ref=fs.at[region], dst_ref=landing(c, 0, (WAVES - 1) * CHUNKS[c]),
            send_sem=ws.at[c], recv_sem=wr.at[c],
            device_id=(z, lax.rem(w + 1, WAVES)), device_id_type=MESH)

    def to_slots(c):
        begin = WAVES * STARTS[c]
        dest, skip = (a_head, 0) if begin < HEAD else (a_tail, HEAD)

        def one(b, carry):
            q = pl.multiple_of(b * 32, 32)
            v = jnp.concatenate([fr[pl.ds(q + 16 * h, 16)].reshape(256, LANES) for h in range(2)], axis=1)
            v = dot(swap[...], v).astype(BF16)
            for h in range(2):
                to = pl.ds(q - skip + 16 * h, 16)
                dest[:, to, :] = v[:, LANES * h : LANES * (h + 1)].reshape(16, 16, LANES)
            return carry

        lax.fori_loop(begin // 32, begin // 32 + CHUNKS[c], one, 0, unroll=min(2, CHUNKS[c]))

    make_table(0, CHUNKS[0])

    leg_copy.wait()

    def order_legendre(s, carry):
        m = wave_s[w * SLOTS + s]
        for h in range(2):
            cols = slice(256 * h, 256 * (h + 1))
            keep = iota((256, 256), 1) + 256 * h >= m
            for q in range(2):
                rows = slice(256 * q, 256 * (q + 1))
                v = dot(onehot[rows, :], lraw[s, :, cols])
                part = lp_head if q == 0 else lp_tail
                part[s, :, cols] = jnp.where(keep, v, 0.0).astype(BF16)
        return carry

    lax.fori_loop(0, SLOTS, order_legendre, 0)

    def arrive(c):
        z_all(c).wait_recv()
        transform(STARTS[c], CHUNKS[c])
        send_wave(c)

    def collect(c):
        wave_all(c).wait_recv()
        to_slots(c)

    make_table(STARTS[1], CHUNKS[1])
    arrive(0)
    make_table(STARTS[2], CHUNKS[2])
    arrive(1)
    make_table(STARTS[3], ROWS - STARTS[3])
    collect(0)
    arrive(2)
    collect(1)

    order = part_last()

    def sum_first(s, carry):
        at = nt_dot(order, a_head[s]).astype(BF16)
        acc[s] = dot(at, lp_head[s])
        return carry

    lax.fori_loop(0, SLOTS, sum_first, 0, unroll=4)

    for c in range(3, LAST + 1):
        arrive(c)
    for c in range(2, LAST):
        collect(c)
    wave_all(LAST).wait_recv()

    for c in range(len(CHUNKS)):
        z_all(c).wait_send()
        wave_all(c).wait_send()


def finish(acc, lp_tail, a_tail, fr, out_hbm, out, a, swap, sems):
    group = 4
    tail = NLAT - HEAD
    ready = CUT - HEAD
    set_swap(swap)
    v = jnp.concatenate([fr[16 * h : 16 * h + 16].reshape(256, LANES) for h in range(2)], axis=1)
    v = dot(swap[...], v).astype(BF16)
    for h in range(2):
        a[:, ready + 16 * h : ready + 16 * h + 16, :] = v[:, LANES * h : LANES * (h + 1)].reshape(16, 16, LANES)
    a[:, :ready, :] = a_tail[...]
    copies = []
    for g in range(SLOTS // group):
        at = nt_dot(part_last(), a[group * g : group * (g + 1)].reshape(group * tail, LANES)).astype(BF16)
        for s in range(group):
            slot = group * g + s
            total = acc[slot] + dot(at[:, tail * s : tail * (s + 1)], lp_tail[slot])
            out[:, slot] = total.astype(BF16).reshape(KEEP, 2, DEG)
        part = pl.ds(group * g, group)
        copies.append(pltpu.make_async_copy(out.at[:, part], out_hbm.at[:, part], sems.at[g]))
        copies[-1].start()
    for copy in copies:
        copy.wait()


def on_device(grid, legendre, lengths, lat_order, wave_order):
    any_spec = pl.BlockSpec(memory_space=pl.ANY)
    vmem = pl.BlockSpec(memory_space=pltpu.VMEM)
    n = len(CHUNKS)
    dma = pltpu.SemaphoreType.DMA
    parts = pl.pallas_call(
        kernel,
        out_shape=[
            pltpu.VMEM((SLOTS, 2 * KEEP, DEG), F32),
            pltpu.VMEM((SLOTS, NLAT - HEAD, DEG), BF16),
            pltpu.VMEM((SLOTS, CUT - HEAD, LANES), BF16),
            pltpu.VMEM((NLAT - CUT, SLOTS, LANES), BF16),
        ],
        in_specs=[any_spec] * 7,
        out_specs=[vmem] * 4,
        scratch_shapes=[
            pltpu.VMEM((512, ROWS, LANES), BF16),
            pltpu.VMEM((LEVS * ROWS, KEEP, LANES), BF16),
            pltpu.VMEM((LEVS * ROWS, KEEP, LANES), BF16),
            pltpu.VMEM((TABLES, 2 * NWAVE, 2 * LANES), BF16),
            pltpu.VMEM((TABLES, 2 * NWAVE, 2 * LANES), F32),
            pltpu.VMEM((2 * NWAVE, 2 * LANES), F32),
            pltpu.VMEM((WAVES * ROWS, SLOTS, LANES), BF16),
            pltpu.VMEM((CUT, SLOTS, LANES), BF16),
            pltpu.VMEM((SLOTS, HEAD, LANES), BF16),
            pltpu.VMEM((SLOTS, NLAT, DEG), BF16),
            pltpu.VMEM((SLOTS, HEAD, DEG), BF16),
            pltpu.VMEM((NLAT, NLAT), BF16),
            pltpu.VMEM((256, 256), BF16),
            pltpu.VMEM((NWAVE, LANES), F32),
            pltpu.SMEM((NLAT,), jnp.int32),
            pltpu.SMEM((NLAT,), jnp.int32),
            pltpu.SMEM((NWAVE,), jnp.int32),
            pltpu.VMEM((4, 128), jnp.int32),
            pltpu.VMEM((4, 128), jnp.int32),
            dma((LEVS,)), dma, dma((5,)), dma((n,)), dma((n,)), dma((n,)), dma((n,)),
        ],
        compiler_params=pltpu.CompilerParams(
            collective_id=0, has_side_effects=True, vmem_limit_bytes=51 << 20
        ),
        cost_estimate=pl.CostEstimate(flops=14 * 10**9, bytes_accessed=14 << 20, transcendentals=0),
    )(grid, legendre, lengths, lat_order, wave_order, lat_order.reshape(4, 128), wave_order.reshape(4, 128))
    return pl.pallas_call(
        finish,
        out_shape=jax.ShapeDtypeStruct((KEEP, SLOTS, 2, DEG), BF16),
        in_specs=[vmem] * 4,
        out_specs=any_spec,
        scratch_shapes=[pltpu.VMEM((KEEP, SLOTS, 2, DEG), BF16), pltpu.VMEM((SLOTS, NLAT - HEAD, LANES), BF16), pltpu.VMEM((256, 256), BF16), dma((4,))],
        compiler_params=pltpu.CompilerParams(vmem_limit_bytes=32 << 20),
    )(*parts)


def solution(mesh):
    return jax.shard_map(
        on_device,
        mesh=mesh,
        in_specs=(P(None, "wave", "lev"), P("wave", None, None), P(), P(), P()),
        out_specs=P("lev", "wave", None, None),
        check_vma=False,
    )
```

```python
import jax
import jax.numpy as jnp
from jax import lax
from jax.experimental import pallas as pl
from jax.experimental.pallas import tpu as pltpu
from jax.sharding import PartitionSpec as P

MESH = pl.DeviceIdType.MESH
BF16 = jnp.bfloat16
F32 = jnp.float32

LEVS = 8
WAVES = 32
ROWS = 16
SLOTS = 16
KEEP = 64
NLAT = 512
DEG = 512
NWAVE = 512
LANES = 128

CHUNKS = (4, 4, 2, 2, 2, 1, 1)
STARTS = tuple(sum(CHUNKS[:i]) for i in range(len(CHUNKS)))
LAST = len(CHUNKS) - 1
CUT = WAVES * STARTS[LAST]
HEAD = 256
TABLES = 8
ZORDER = (4, 3, 5, 2, 6, 1, 7)

SIN_C = (3.14159264, -5.16771008, 2.55007752, -0.59829129, 0.07765766)
COS_C = (0.99999995, -4.93479283, 4.05841135, -1.33187657, 0.21968961)


def iota(shape, dim):
    return lax.broadcasted_iota(jnp.int32, shape, dim)


def horner(coefs, u):
    acc = u * coefs[-1] + coefs[-2]
    for c in coefs[-3::-1]:
        acc = acc * u + c
    return acc


def turn(count, width, inverse):
    whole = jnp.floor(count * inverse + 0.5)
    t = (count - whole * width) * inverse
    u = t * t
    s = t * horner(SIN_C, u)
    c = horner(COS_C, u)
    s2 = s + s
    return 1.0 - s2 * s, s2 * c


def nt_dot(a, b):
    return lax.dot_general(a, b, (((1,), (1,)), ((), ())), preferred_element_type=F32)


def dot(a, b):
    return jnp.dot(a, b, preferred_element_type=F32)


def set_swap(swap):
    i = iota((256, 256), 0)
    j = iota((256, 256), 1)
    swap[...] = jnp.where(j == (i & 15) * 16 + (i >> 4), 1.0, 0.0).astype(BF16)


def part_last():
    i = iota((LANES, LANES), 0)
    j = iota((LANES, LANES), 1)
    return jnp.where(j == (i & 1) * KEEP + (i >> 1), 1.0, 0.0).astype(BF16)


def kernel(grid_hbm, leg_hbm, len_hbm, lat_hbm, wave_hbm, lat4_hbm, wave4_hbm, acc, lp_tail, a_tail, fr_last,
           gin, g, x, table, turns, both, fs, fr, a_head, lraw, lp_head, onehot, swap, mcol,
           len_s, lat_s, wave_s, lat_v, wave_v, gin_sem, leg_sem, small_sem, zs, zr, ws, wr):
    z = lax.axis_index("lev")
    w = lax.axis_index("wave")
    bar = pltpu.get_barrier_semaphore()

    def signal_z(i, carry):
        pl.semaphore_signal(bar, inc=1, device_id=(lax.rem(z + i, LEVS), w), device_id_type=MESH)
        return carry

    def signal_w(i, carry):
        pl.semaphore_signal(bar, inc=1, device_id=(z, lax.rem(w + i, WAVES)), device_id_type=MESH)
        return carry

    visit = ZORDER + (0,)

    def grid_copy(i):
        part = pl.ds(lax.rem(z + visit[i], LEVS) * KEEP, KEEP)
        return pltpu.make_async_copy(grid_hbm.at[part], gin.at[part], gin_sem.at[i])

    for i in range(LEVS):
        grid_copy(i).start()
    lax.fori_loop(1, LEVS, signal_z, 0)
    lax.fori_loop(1, WAVES, signal_w, 0)
    small = [
        pltpu.make_async_copy(src, dst, small_sem.at[i])
        for i, (src, dst) in enumerate(
            [(len_hbm, len_s), (lat_hbm, lat_s), (wave_hbm, wave_s), (lat4_hbm, lat_v), (wave4_hbm, wave_v)]
        )
    ]
    for copy in small:
        copy.start()
    leg_copy = pltpu.make_async_copy(leg_hbm, lraw, leg_sem)
    leg_copy.start()

    set_swap(swap)

    def send_z(c, p):
        rows = CHUNKS[c]
        base = LEVS * STARTS[c]
        pltpu.make_async_remote_copy(
            src_ref=g.at[pl.ds(base + p * rows, rows)],
            dst_ref=x.at[pl.ds(base + z * rows, rows)],
            send_sem=zs.at[c], recv_sem=zr.at[c],
            device_id=(p, w), device_id_type=MESH,
        ).start()

    for i in range(LEVS):
        grid_copy(i).wait()
        p = lax.rem(z + visit[i], LEVS)
        for pair in range(2):
            k0 = pl.multiple_of(p * KEEP + pair * 32, 32)
            v = jnp.concatenate([gin[pl.ds(k0 + 16 * h, 16)].reshape(256, LANES) for h in range(2)], axis=1)
            v = dot(swap[...], v).astype(BF16)
            for h in range(2):
                kk = pair * 32 + 16 * h
                part = v[:, LANES * h : LANES * (h + 1)].reshape(16, 16, LANES)
                for c, rows in enumerate(CHUNKS):
                    r0 = STARTS[c]
                    dest = g if i < LEVS - 1 else x
                    dest[pl.ds(LEVS * r0 + p * rows, rows), kk : kk + 16, :] = part[r0 : r0 + rows]
        if i == 0:
            pl.semaphore_wait(bar, LEVS - 1 + WAVES - 1)
        if i < LEVS - 1:
            send_z(0, p)
    for c in range(1, len(CHUNKS)):
        for o in ZORDER:
            send_z(c, lax.rem(z + o, LEVS))

    for copy in small:
        copy.wait()
    col = jnp.zeros((NWAVE, LANES), F32)
    for t in range(4):
        hit = iota((NWAVE, LANES), 1) + LANES * t == iota((NWAVE, LANES), 0)
        col = col + jnp.where(hit, wave_v[t : t + 1, :].astype(F32), 0.0)
    mcol[...] = jnp.broadcast_to(jnp.sum(col, axis=1, keepdims=True), (NWAVE, LANES))
    for c, rows in enumerate(CHUNKS):
        n = WAVES * rows
        q = iota((n, LANES), 0)
        row = (q // rows) * ROWS + STARTS[c] + q % rows
        col = jnp.zeros((n, LANES), F32)
        for t in range(4):
            hit = iota((n, LANES), 1) + LANES * t == row
            col = col + jnp.where(hit, lat_v[t : t + 1, :].astype(F32), 0.0)
        lat = jnp.sum(col, axis=1, keepdims=True)
        onehot[WAVES * STARTS[c] : WAVES * STARTS[c] + n, :] = jnp.where(
            iota((n, NLAT), 1).astype(F32) == lat, 1.0, 0.0
        ).astype(BF16)

    def make_table(r0, rows):
        def one(rr, carry):
            held = r0 % TABLES + rr
            length = len_s[lat_s[w * ROWS + r0 + rr]]
            width = jnp.full((1, LANES), length, jnp.int32).astype(F32)
            inverse = 1.0 / width
            factor = 1.0 / jnp.sqrt(width)
            lane = iota((32, LANES), 1)
            left = lane < KEEP
            low = lane.astype(F32)

            def block(b, carry2):
                s0 = pl.multiple_of(b * 32, 32)
                rows_c = pl.ds(s0, 32)
                rows_s = pl.ds(NWAVE + s0, 32)
                m = mcol[rows_c, :]
                cl, sl = turn(m * low, width, inverse)
                table[held, rows_c, :LANES] = cl.astype(BF16)
                table[held, rows_s, :LANES] = sl.astype(BF16)
                c1, s1 = turn(m * float(LANES), width, inverse)
                table[held, rows_c, LANES:] = (cl * c1 - sl * s1).astype(BF16)
                table[held, rows_s, LANES:] = (sl * c1 + cl * s1).astype(BF16)
                t = s1 + s1
                c2, s2 = 1.0 - t * s1, t * c1
                t = s2 + s2
                c4, s4 = factor - t * (s2 * factor), t * (c2 * factor)
                turns[held, rows_c, :LANES] = jnp.where(left, 1.0, c2) * factor
                turns[held, rows_s, :LANES] = jnp.where(left, 0.0, s2) * factor
                turns[held, rows_c, LANES:] = jnp.where(left, c4, c4 * c2 - s4 * s2)
                turns[held, rows_s, LANES:] = jnp.where(left, s4, s4 * c2 + c4 * s2)
                return carry2

            lax.fori_loop(0, NWAVE // 32, block, 0, unroll=2)
            return carry

        lax.fori_loop(0, rows, one, 0)

    def transform(r0, rows):
        left = iota((32, LANES), 1) < KEEP

        def one(rr, carry):
            length = len_s[lat_s[w * ROWS + r0 + rr]]
            held = r0 % TABLES + rr
            parts = []
            for d in range(LEVS):
                inside = iota((KEEP, LANES), 1) + d * LANES < length
                keep = jnp.where(inside, 1.0, 0.0).astype(BF16)
                parts.append(x[LEVS * r0 + d * rows + rr] * keep)
            lines = jnp.concatenate(
                [jnp.concatenate(parts[2 * d : 2 * d + 2], axis=1) for d in range(4)], axis=0
            )
            both[...] = nt_dot(table[held], lines)
            for b in range(NWAVE // 32):
                rows_c = slice(32 * b, 32 * (b + 1))
                rows_s = slice(NWAVE + 32 * b, NWAVE + 32 * (b + 1))
                real, imag = 0.0, 0.0
                for t in range(2):
                    cols = slice(LANES * t, LANES * (t + 1))
                    u, v = both[rows_c, cols], both[rows_s, cols]
                    c, q = turns[held, rows_c, cols], turns[held, rows_s, cols]
                    real = real + (c * u - q * v)
                    imag = imag - (q * u + c * v)
                f = jnp.where(left, real, pltpu.roll(imag, KEEP, axis=1))
                f = f + jnp.where(left, pltpu.roll(real, KEEP, axis=1), imag)
                f = f.astype(BF16)
                for i in range(2):
                    fs[WAVES * r0 + (2 * b + i) * rows + rr] = f[SLOTS * i : SLOTS * (i + 1)]
            return carry

        lax.fori_loop(0, rows, one, 0)

    def landing(c, first, count):
        if c == LAST:
            return fr_last.at[pl.ds(first, count)]
        return fr.at[pl.ds(WAVES * STARTS[c] + first, count)]

    def send_wave(c):
        rows = CHUNKS[c]
        base = WAVES * STARTS[c]

        def one(o, carry):
            px = lax.rem(w // 8 + o // 8, 4)
            py = lax.rem(lax.rem(w // 2, 4) + lax.rem(o // 2, 4), 4)
            pc = lax.rem(lax.rem(w, 2) + lax.rem(o, 2), 2)
            p = px * 8 + py * 2 + pc
            pltpu.make_async_remote_copy(
                src_ref=fs.at[pl.ds(base + p * rows, rows)],
                dst_ref=landing(c, w * rows, rows),
                send_sem=ws.at[c], recv_sem=wr.at[c],
                device_id=(z, p), device_id_type=MESH,
            ).start()
            return carry

        lax.fori_loop(1, WAVES, one, 0, unroll=c == LAST)
        own = pl.ds(base + w * rows, rows)
        if c == LAST:
            fr_last[pl.ds(w * rows, rows)] = fs[own]
        else:
            fr[own] = fs[own]

    def z_all(c):
        region = pl.ds(LEVS * STARTS[c], (LEVS - 1) * CHUNKS[c])
        return pltpu.make_async_remote_copy(
            src_ref=g.at[region], dst_ref=x.at[region], send_sem=zs.at[c], recv_sem=zr.at[c],
            device_id=(lax.rem(z + 1, LEVS), w), device_id_type=MESH)

    def wave_all(c):
        region = pl.ds(WAVES * STARTS[c], (WAVES - 1) * CHUNKS[c])
        return pltpu.make_async_remote_copy(
            src_ref=fs.at[region], dst_ref=landing(c, 0, (WAVES - 1) * CHUNKS[c]),
            send_sem=ws.at[c], recv_sem=wr.at[c],
            device_id=(z, lax.rem(w + 1, WAVES)), device_id_type=MESH)

    def to_slots(c):
        begin = WAVES * STARTS[c]
        dest, skip = (a_head, 0) if begin < HEAD else (a_tail, HEAD)

        def one(b, carry):
            q = pl.multiple_of(b * 32, 32)
            v = jnp.concatenate([fr[pl.ds(q + 16 * h, 16)].reshape(256, LANES) for h in range(2)], axis=1)
            v = dot(swap[...], v).astype(BF16)
            for h in range(2):
                to = pl.ds(q - skip + 16 * h, 16)
                dest[:, to, :] = v[:, LANES * h : LANES * (h + 1)].reshape(16, 16, LANES)
            return carry

        lax.fori_loop(begin // 32, begin // 32 + CHUNKS[c], one, 0, unroll=min(2, CHUNKS[c]))

    make_table(0, CHUNKS[0])

    leg_copy.wait()

    def order_legendre(s, carry):
        m = wave_s[w * SLOTS + s]
        for h in range(2):
            cols = slice(256 * h, 256 * (h + 1))
            keep = iota((256, 256), 1) + 256 * h >= m
            for q in range(2):
                rows = slice(256 * q, 256 * (q + 1))
                v = dot(onehot[rows, :], lraw[s, :, cols])
                part = lp_head if q == 0 else lp_tail
                part[s, :, cols] = jnp.where(keep, v, 0.0).astype(BF16)
        return carry

    lax.fori_loop(0, SLOTS, order_legendre, 0)

    def arrive(c):
        z_all(c).wait_recv()
        transform(STARTS[c], CHUNKS[c])
        send_wave(c)

    def collect(c):
        wave_all(c).wait_recv()
        to_slots(c)

    make_table(STARTS[1], CHUNKS[1])
    arrive(0)
    make_table(STARTS[2], CHUNKS[2])
    arrive(1)
    make_table(STARTS[3], ROWS - STARTS[3])
    collect(0)
    arrive(2)
    arrive(3)
    collect(1)

    order = part_last()

    def sum_first(s, carry):
        at = nt_dot(order, a_head[s]).astype(BF16)
        acc[s] = dot(at, lp_head[s])
        return carry

    lax.fori_loop(0, SLOTS, sum_first, 0, unroll=4)

    for c in range(4, LAST + 1):
        arrive(c)
    for c in range(2, LAST):
        collect(c)
    wave_all(LAST).wait_recv()

    for c in range(len(CHUNKS)):
        z_all(c).wait_send()
        wave_all(c).wait_send()


def finish(acc, lp_tail, a_tail, fr, out_hbm, out, a, swap, sems):
    group = 4
    tail = NLAT - HEAD
    ready = CUT - HEAD
    set_swap(swap)
    v = jnp.concatenate([fr[16 * h : 16 * h + 16].reshape(256, LANES) for h in range(2)], axis=1)
    v = dot(swap[...], v).astype(BF16)
    for h in range(2):
        a[:, ready + 16 * h : ready + 16 * h + 16, :] = v[:, LANES * h : LANES * (h + 1)].reshape(16, 16, LANES)
    a[:, :ready, :] = a_tail[...]
    copies = []
    for g in range(SLOTS // group):
        at = nt_dot(part_last(), a[group * g : group * (g + 1)].reshape(group * tail, LANES)).astype(BF16)
        for s in range(group):
            slot = group * g + s
            total = acc[slot] + dot(at[:, tail * s : tail * (s + 1)], lp_tail[slot])
            out[:, slot] = total.astype(BF16).reshape(KEEP, 2, DEG)
        part = pl.ds(group * g, group)
        copies.append(pltpu.make_async_copy(out.at[:, part], out_hbm.at[:, part], sems.at[g]))
        copies[-1].start()
    for copy in copies:
        copy.wait()


def on_device(grid, legendre, lengths, lat_order, wave_order):
    any_spec = pl.BlockSpec(memory_space=pl.ANY)
    vmem = pl.BlockSpec(memory_space=pltpu.VMEM)
    n = len(CHUNKS)
    dma = pltpu.SemaphoreType.DMA
    parts = pl.pallas_call(
        kernel,
        out_shape=[
            pltpu.VMEM((SLOTS, 2 * KEEP, DEG), F32),
            pltpu.VMEM((SLOTS, NLAT - HEAD, DEG), BF16),
            pltpu.VMEM((SLOTS, CUT - HEAD, LANES), BF16),
            pltpu.VMEM((NLAT - CUT, SLOTS, LANES), BF16),
        ],
        in_specs=[any_spec] * 7,
        out_specs=[vmem] * 4,
        scratch_shapes=[
            pltpu.VMEM((512, ROWS, LANES), BF16),
            pltpu.VMEM((LEVS * ROWS, KEEP, LANES), BF16),
            pltpu.VMEM((LEVS * ROWS, KEEP, LANES), BF16),
            pltpu.VMEM((TABLES, 2 * NWAVE, 2 * LANES), BF16),
            pltpu.VMEM((TABLES, 2 * NWAVE, 2 * LANES), F32),
            pltpu.VMEM((2 * NWAVE, 2 * LANES), F32),
            pltpu.VMEM((WAVES * ROWS, SLOTS, LANES), BF16),
            pltpu.VMEM((CUT, SLOTS, LANES), BF16),
            pltpu.VMEM((SLOTS, HEAD, LANES), BF16),
            pltpu.VMEM((SLOTS, NLAT, DEG), BF16),
            pltpu.VMEM((SLOTS, HEAD, DEG), BF16),
            pltpu.VMEM((NLAT, NLAT), BF16),
            pltpu.VMEM((256, 256), BF16),
            pltpu.VMEM((NWAVE, LANES), F32),
            pltpu.SMEM((NLAT,), jnp.int32),
            pltpu.SMEM((NLAT,), jnp.int32),
            pltpu.SMEM((NWAVE,), jnp.int32),
            pltpu.VMEM((4, 128), jnp.int32),
            pltpu.VMEM((4, 128), jnp.int32),
            dma((LEVS,)), dma, dma((5,)), dma((n,)), dma((n,)), dma((n,)), dma((n,)),
        ],
        compiler_params=pltpu.CompilerParams(
            collective_id=0, has_side_effects=True, vmem_limit_bytes=51 << 20
        ),
        cost_estimate=pl.CostEstimate(flops=14 * 10**9, bytes_accessed=14 << 20, transcendentals=0),
    )(grid, legendre, lengths, lat_order, wave_order, lat_order.reshape(4, 128), wave_order.reshape(4, 128))
    return pl.pallas_call(
        finish,
        out_shape=jax.ShapeDtypeStruct((KEEP, SLOTS, 2, DEG), BF16),
        in_specs=[vmem] * 4,
        out_specs=any_spec,
        scratch_shapes=[pltpu.VMEM((KEEP, SLOTS, 2, DEG), BF16), pltpu.VMEM((SLOTS, NLAT - HEAD, LANES), BF16), pltpu.VMEM((256, 256), BF16), dma((4,))],
        compiler_params=pltpu.CompilerParams(vmem_limit_bytes=32 << 20),
    )(*parts)


def solution(mesh):
    return jax.shard_map(
        on_device,
        mesh=mesh,
        in_specs=(P(None, "wave", "lev"), P("wave", None, None), P(), P(), P()),
        out_specs=P("lev", "wave", None, None),
        check_vma=False,
    )
```
